256 devices in a mesh: vox: 64 (over z, y, core), frm: 4 (over x).
Axes of the slice: x: 4, y: 4, z: 8, core: 2. Of those that a mesh axis runs over, the one named last changes fastest.
Arguments:
- data: bfloat16 [262144, 1024], P('vox', 'frm'), may hold values from -6 to 10.375
- footprints: bfloat16 [512, 4, 512, 128], P('vox'), may hold values from 0 to 1, as said below
- traces: bfloat16 [512, 128, 1024], P('vox', None, 'frm'), may hold values from 0 to 1
- incidence: int32 [512, 4], replicated, may hold values from 0 to 511, as said below
- counts: int32 [512], replicated, may hold values from 1 to 128
Outputs:
- new_traces: bfloat16 [512, 128, 1024], P('vox', None, 'frm')
- new_footprints: bfloat16 [512, 4, 512, 128], P('vox', None, 'frm')
The draws below stay inside these ranges and needn't reach their ends.
Inputs may be any that keep to these rules, and one draw needn't show every extreme that they name: `incidence`: neuron block j is owned by the device of vox index j // 8. Among the 32 entries of one device's voxel blocks, at most 1 name blocks of one owner, and exactly 1 do for some owner. Over all devices, the blocks of each owner are named exactly 8 * 4 times, and every neuron block is named at least once. `footprints`: every entry is 0 or positive; every neuron column of every tile has a positive entry.
All inputs are finite; a program needn't handle non-finite values.
Results may differ from the reference program's by a relative error of at most 0.0034.
Values may be sent and summed in bfloat16 or wider, within the bound.
No kernel may reach another device: no remote copies, remote signals or barrier semaphores. Data moves between devices by JAX's collectives and lax.ppermute only.
A program may use at most 128 MiB of HBM per device.

```python
import math
import jax
import jax.numpy as jnp
from jax import lax

BV = 512
BN = 128
K = 4
VB_DEV = 8
NB_DEV = 8
VBLOCKS = 512
NBLOCKS = 512
VOXELS = 262144
FRAMES = 1024
CAP = 1
N_VOX = 64


def draw_footprints(key, part):
    key_value, key_spread, key_pinned = jax.random.split(key, 3)
    shape = (VBLOCKS, K, BV, BN)
    values = jnp.exp(jax.random.uniform(key_value, shape, jnp.float32, math.log(0.25), 0.0))
    spread = jax.random.uniform(key_spread, shape, jnp.float32) < 1.0 / 32.0
    pinned = jax.random.randint(key_pinned, (VBLOCKS, K, 1, BN), 0, BV)
    voxel_rows = jnp.arange(BV, dtype=jnp.int32)[None, None, :, None]
    return jnp.where(spread | (voxel_rows == pinned), values, 0.0).astype(jnp.bfloat16)


def draw_incidence(key, part):
    key_first, key_pool, key_shift, key_order = jax.random.split(key, 4)
    entries = VB_DEV * K
    pool_size = N_VOX * CAP
    position = jnp.arange(pool_size, dtype=jnp.int32)
    pool = position % N_VOX
    first = jax.random.randint(key_first, (), 0, N_VOX)
    shuffled = jax.random.permutation(key_pool, pool_size).astype(jnp.int32)
    wanted = (pool == 1) | (pool == N_VOX - 1) | (pool == N_VOX // 2)
    forced = wanted & (position < N_VOX) & (pool != first)
    scores = jnp.where(pool == first, position, jnp.where(forced, pool_size + position, 2 * pool_size + shuffled))
    ranking = jnp.argsort(scores)
    offsets = pool[ranking[:entries]]
    shifts = jax.random.randint(key_shift, (N_VOX,), 0, NB_DEV)
    source = jnp.arange(N_VOX, dtype=jnp.int32)[:, None]
    owners = (source + offsets[None, :]) % N_VOX
    entry_index = jnp.arange(entries, dtype=jnp.int32)[None, :]
    within = (entry_index + shifts[owners]) % NB_DEV
    named = owners * NB_DEV + within
    row_keys = jax.random.split(key_order, N_VOX)

    def shuffle_row(subkey):
        return jax.random.permutation(subkey, entries)
    orders = jax.vmap(shuffle_row)(row_keys).astype(jnp.int32)
    placed = jnp.take_along_axis(named, orders, axis=1)
    return placed.reshape(VBLOCKS, K).astype(jnp.int32)


def set_ends(drawn, own_key, smallest, largest):
    longest = drawn.shape.index(max(drawn.shape))
    spots = []
    for shift in (0, 1):
        where = [jax.random.randint(jax.random.fold_in(own_key, axis), (), 0, length) for axis, length in enumerate(drawn.shape)]
        where[longest] = (where[longest] + shift) % drawn.shape[longest]
        spots.append(tuple(where))
    return drawn.at[spots[0]].set(smallest).at[spots[1]].set(largest)


def shard_levels(stream_key, shape, cuts, smallest, largest):
    def one(dim, shards_of):
        heights = jax.random.uniform(jax.random.fold_in(jax.random.fold_in(stream_key, 6), dim), (shards_of,), jnp.float32, smallest / len(cuts), largest / len(cuts))
        return jnp.repeat(jnp.exp(heights), shape[dim] // shards_of).reshape((-1,) + (1,) * (len(shape) - dim - 1))

    loudness = one(*cuts[0])
    for cut in cuts[1:]:
        loudness = loudness * one(*cut)
    return loudness


def setup_inputs(seed: int = 0) -> dict:
    seeds = jax.random.split(jax.random.key(seed), 6)
    return {
        "data": jnp.clip(-6.0 + 16.375 * jax.random.uniform(seeds[0], (VOXELS, FRAMES), jnp.float32) ** shard_levels(seeds[0], (VOXELS, FRAMES), ((0, 64), (1, 4)), -0.2, 0.2), -6.0, 10.375).astype(jnp.bfloat16),
        "footprints": draw_footprints(jax.random.fold_in(seeds[5], 71), 0),
        "traces": jnp.clip(1.0 * jax.random.uniform(seeds[2], (NBLOCKS, BN, FRAMES), jnp.float32) ** shard_levels(seeds[2], (NBLOCKS, BN, FRAMES), ((0, 64), (2, 4)), -0.2, 0.2), 0.0, 1.0).astype(jnp.bfloat16),
        "incidence": draw_incidence(jax.random.fold_in(seeds[5], 71), 0),
        "counts": set_ends(jax.random.randint(seeds[4], (NBLOCKS,), 1, BN + 1), jax.random.fold_in(seeds[4], 1), 1, BN).astype(jnp.int32),
    }


highest = lax.Precision.HIGHEST


def reference(data, footprints, traces, incidence, counts):
    neuron = jnp.arange(BN, dtype=jnp.int32)
    live = neuron[None, :] < counts[:, None]
    alive = jnp.where(live[:, :, None], traces, jnp.zeros((), traces.dtype))
    blocks = data.reshape(VBLOCKS, BV, FRAMES)

    def residual(vblock, source):
        picked = source[incidence[vblock]]
        recon = jnp.einsum('kxn,knf->xf', footprints[vblock].astype(jnp.float32), picked.astype(jnp.float32), precision=highest)
        resid = (blocks[vblock].astype(jnp.float32) - recon).astype(jnp.bfloat16)
        return resid, picked

    def trace_step(carry, vblock):
        grad, denom = carry
        resid, unused = residual(vblock, alive)
        tiles = footprints[vblock].astype(jnp.float32)
        term = jnp.einsum('kxn,xf->knf', tiles, resid.astype(jnp.float32), precision=highest)
        rowsum = jnp.sum(tiles, axis=(0, 2))
        dterm = jnp.einsum('kxn,x->kn', tiles, rowsum, precision=highest)
        named = incidence[vblock]
        return (grad.at[named].add(term), denom.at[named].add(dterm)), None

    start = (jnp.zeros((NBLOCKS, BN, FRAMES), jnp.float32), jnp.zeros((NBLOCKS, BN), jnp.float32))
    (grad, denom), unused = lax.scan(trace_step, start, jnp.arange(VBLOCKS, dtype=jnp.int32))
    updated = jnp.maximum(traces.astype(jnp.float32) + grad / denom[:, :, None], 0.0)
    new_traces = jnp.where(live[:, :, None], updated, 0.0).astype(jnp.bfloat16)

    def foot_step(vblock):
        resid, picked = residual(vblock, new_traces)
        fgrad = jnp.einsum('xf,knf->kxn', resid.astype(jnp.float32), picked.astype(jnp.float32), precision=highest)
        power = jnp.sum(jnp.square(picked.astype(jnp.float32)), axis=2)
        tiles = footprints[vblock]
        keep = live[incidence[vblock]][:, None, :] & (tiles > 0)
        moved = jnp.maximum(tiles.astype(jnp.float32) + fgrad / jnp.maximum(power, 1.0)[:, None, :], 0.0)
        return jnp.where(keep, moved, 0.0).astype(jnp.bfloat16)

    new_footprints = lax.map(foot_step, jnp.arange(VBLOCKS, dtype=jnp.int32))
    return new_traces, new_footprints
```

```python
import functools

import jax
import jax.numpy as jnp
from jax import lax
from jax.experimental import pallas as pl
from jax.experimental.pallas import tpu as pltpu
from jax.sharding import Mesh
from jax.sharding import PartitionSpec as P

NZ, NY, NC, NX = 8, 4, 2, 4
PLANE = NY * NC
OWNED = 8
BN = 128
BV = 512
K = 4
VB = 8
ENTRIES = VB * K
W = 128
CHUNKS = 2
VLOC = VB // NX
ELOC = VLOC * K

VM = pl.BlockSpec(memory_space=pltpu.VMEM)
SM = pl.BlockSpec(memory_space=pltpu.SMEM)
highest = lax.Precision.HIGHEST


def params(mib):
    return pltpu.CompilerParams(vmem_limit_bytes=mib * 2**20)


def cost(flops, nbytes):
    return pl.CostEstimate(flops=flops, bytes_accessed=nbytes, transcendentals=0)


def whole_call(kernel, out_shape, n_smem, n_vmem, scratch, mib, nbytes):
    out_specs = [VM] * len(out_shape)
    return pl.pallas_call(
        kernel,
        out_shape=out_shape,
        in_specs=[SM] * n_smem + [VM] * n_vmem,
        out_specs=out_specs,
        scratch_shapes=scratch,
        compiler_params=params(mib),
        cost_estimate=cost(0, nbytes),
    )


def blocks(n):
    return jax.ShapeDtypeStruct((n, BN, W), jnp.bfloat16)


def select_kernel(sel, where, own, p1, p2, p3, p4, m1, m2, m3, m4, *outs):
    by_r = (own, m1, m2, m3, None, p3, p2, p1)
    half = OWNED // 2
    for s in range(PLANE):
        q = jnp.bitwise_xor(where[0], s)
        for r in range(NZ):
            b = jnp.maximum(sel[q * NZ + r], 0)
            if r == NZ // 2:
                low = b < half

                @pl.when(low)
                def _():
                    outs[s][r] = p4[b]

                @pl.when(jnp.logical_not(low))
                def _():
                    outs[s][r] = m4[b - half]
            else:
                outs[s][r] = by_r[r][b]


def select(sel, where, ring):
    call = whole_call(select_kernel, [blocks(NZ)] * PLANE, 2, len(ring), [], 16, 4 << 20)
    return call(sel, where, *ring)


def slot_of(j, where):
    owner = lax.shift_right_logical(j, 3)
    s = jnp.bitwise_xor(jnp.bitwise_and(owner, PLANE - 1), where[0])
    r = jnp.bitwise_and(lax.shift_right_logical(owner, 3) - where[1], NZ - 1)
    return s * NZ + r


def prep_kernel(f_ref, ft_ref, d_ref):
    rowsum = jnp.zeros((BV, 1), jnp.float32)
    for k in range(K):
        tile = f_ref[0, k]
        ft_ref[0, k] = tile.T
        rowsum = rowsum + jnp.sum(tile.astype(jnp.float32), axis=1, keepdims=True)
    for k in range(K):
        d_ref[0, k : k + 1, :] = jnp.sum(
            f_ref[0, k].astype(jnp.float32) * rowsum, axis=0, keepdims=True
        )


def prep(footprints):
    return pl.pallas_call(
        prep_kernel,
        grid=(VB,),
        in_specs=[pl.BlockSpec((1, K, BV, BN), lambda v: (v, 0, 0, 0))],
        out_specs=[
            pl.BlockSpec((1, K, BN, BV), lambda v: (v, 0, 0, 0)),
            pl.BlockSpec((1, K, BN), lambda v: (v, 0, 0)),
        ],
        out_shape=[
            jax.ShapeDtypeStruct((VB, K, BN, BV), jnp.bfloat16),
            jax.ShapeDtypeStruct((VB, K, BN), jnp.float32),
        ],
        compiler_params=params(16),
        cost_estimate=cost(4 * VB * K * BV * BN, 8 << 20),
    )(footprints)


def terms_kernel(inc, counts, ent, where, d_ref, f_ref, ft_ref, *rest):
    arrived = rest[:PLANE]
    outs = rest[PLANE : 2 * PLANE]
    held, made = rest[2 * PLANE :]
    v = pl.program_id(0)

    @pl.when(v == 0)
    def _():
        for s in range(PLANE):
            held[s * NZ : (s + 1) * NZ] = arrived[s][...]

    neuron = lax.broadcasted_iota(jnp.int32, (BN, W), 0)
    parts = []
    for k in range(K):
        j = inc[v * K + k]
        got = held[slot_of(j, where)]
        parts.append(jnp.where(neuron < counts[j], got, jnp.zeros((), jnp.bfloat16)))
    t_cat = jnp.concatenate(parts, axis=0)
    f_cat = jnp.concatenate([f_ref[0, k] for k in range(K)], axis=1)
    recon = jnp.dot(f_cat, t_cat, preferred_element_type=jnp.float32)
    resid = (d_ref[...].astype(jnp.float32) - recon).astype(jnp.bfloat16)
    ft_cat = ft_ref[0].reshape(K * BN, BV)
    term = jnp.dot(ft_cat, resid, preferred_element_type=jnp.float32)
    made[pl.ds(v * K, K)] = term.astype(jnp.bfloat16).reshape(K, BN, W)

    @pl.when(v == VB - 1)
    def _():
        for s in range(PLANE):
            q = jnp.bitwise_xor(where[0], s)
            for r in range(NZ):
                outs[s][r] = made[ent[q * NZ + r]]


def terms(chunk, inc, counts, ent, where, data, footprints, flipped, arrived):
    whole = pl.BlockSpec((NZ, BN, W), lambda v: (0, 0, 0))
    return pl.pallas_call(
        terms_kernel,
        grid=(VB,),
        in_specs=[SM] * 4
        + [
            pl.BlockSpec((BV, W), lambda v: (v, chunk)),
            pl.BlockSpec((1, K, BV, BN), lambda v: (v, 0, 0, 0)),
            pl.BlockSpec((1, K, BN, BV), lambda v: (v, 0, 0, 0)),
        ]
        + [whole] * PLANE,
        out_specs=[whole] * PLANE,
        out_shape=[blocks(NZ)] * PLANE,
        scratch_shapes=[
            pltpu.VMEM((PLANE * NZ, BN, W), jnp.bfloat16),
            pltpu.VMEM((ENTRIES, BN, W), jnp.bfloat16),
        ],
        compiler_params=params(24),
        cost_estimate=cost(4 * VB * BV * K * BN * W, 13 << 20),
    )(inc, counts, ent, where, data, footprints, flipped, *arrived)


def sum_kernel(sel, where, *refs):
    arrived = refs[:PLANE]
    outs = refs[PLANE : PLANE + NZ]
    total = refs[PLANE + NZ]
    for r in range(NZ):
        total[...] = jnp.zeros_like(total)
        for s in range(PLANE):
            b = sel[jnp.bitwise_xor(where[0], s) * NZ + r]

            @pl.when(b >= 0)
            def _():
                total[b] += arrived[s][r].astype(jnp.float32)

        outs[r][...] = total[...].astype(outs[r].dtype)


def sum_terms(sel, where, arrived):
    shapes = [jax.ShapeDtypeStruct((OWNED, BN, W), jnp.float32)] + [blocks(OWNED)] * (NZ - 1)
    scratch = [pltpu.VMEM((OWNED, BN, W), jnp.float32)]
    return whole_call(sum_kernel, shapes, 2, PLANE, scratch, 16, 5 << 20)(sel, where, *arrived)


def pack_kernel(inc, where, *refs):
    arrived = refs[:PLANE]
    outs = refs[PLANE : PLANE + NX]
    held = refs[PLANE + NX]
    for s in range(PLANE):
        held[s * NZ : (s + 1) * NZ] = arrived[s][...]
    for t in range(NX):
        first = jnp.bitwise_xor(where[2], t) * ELOC
        for i in range(ELOC):
            outs[t][i] = held[slot_of(inc[first + i], where)]


def pack(inc, where, arrived):
    scratch = [pltpu.VMEM((PLANE * NZ, BN, W), jnp.bfloat16)]
    return whole_call(pack_kernel, [blocks(ELOC)] * NX, 2, PLANE, scratch, 16, 3 << 20)(
        inc, where, *arrived
    )


def foot_kernel(inc, counts, where, f_ref, *refs):
    movies = refs[:NX]
    sources = [refs[NX + c * NX : NX + (c + 1) * NX] for c in range(CHUNKS)]
    outs = refs[NX + CHUNKS * NX : NX + CHUNKS * NX + NX]
    total, moved = refs[NX + CHUNKS * NX + NX :]
    i = pl.program_id(0)
    f_cat = jnp.concatenate([f_ref[0, k] for k in range(K)], axis=1)
    powers = [jnp.zeros((BN, 1), jnp.float32) for _ in range(K)]
    for t in range(NX):
        wide = []
        for k in range(K):
            row = jnp.concatenate([sources[c][t][i * K + k] for c in range(CHUNKS)], axis=1)
            row32 = row.astype(jnp.float32)
            powers[k] = powers[k] + jnp.sum(row32 * row32, axis=1, keepdims=True)
            wide.append(row)
        t_cat = jnp.concatenate(wide, axis=0)
        recon = jnp.dot(f_cat, t_cat, preferred_element_type=jnp.float32)
        movie = movies[t][...]
        resid = (movie.astype(jnp.float32) - recon).astype(jnp.bfloat16)
        part = lax.dot_general(
            resid, t_cat, (((1,), (1,)), ((), ())), preferred_element_type=jnp.float32
        )
        if t == 0:
            total[...] = part
        else:
            total[...] += part
    neuron = lax.broadcasted_iota(jnp.int32, (1, BN), 1)
    for k in range(K):
        power = jnp.broadcast_to(powers[k], (BN, BN)).T[0:1, :]
        alive = neuron < counts[inc[where[2] * ELOC + i * K + k]]
        tile = f_ref[0, k]
        fgrad = total[:, k * BN : (k + 1) * BN]
        tile32 = tile.astype(jnp.float32)
        new = jnp.maximum(tile32 + fgrad / jnp.maximum(power, 1.0), 0.0)
        keep = jnp.logical_and(tile32 > 0, alive)
        moved[k] = jnp.where(keep, new, 0.0).astype(jnp.bfloat16)
    rows = BV // NX
    for t in range(NX):
        start = pl.multiple_of(jnp.bitwise_xor(where[2], t) * rows, rows)
        outs[t][0] = moved[:, pl.ds(start, rows), :]


def foot(inc, counts, where, footprints, movies, sources):
    rows = BV // NX
    whole = pl.BlockSpec((ELOC, BN, W), lambda i, *s: (0, 0, 0))
    out = pl.BlockSpec((1, K, rows, BN), lambda i, *s: (i, 0, 0, 0))
    spec = pltpu.PrefetchScalarGridSpec(
        num_scalar_prefetch=3,
        grid=(VLOC,),
        in_specs=[
            pl.BlockSpec((1, K, BV, BN), lambda i, inc, counts, where: (where[2] * VLOC + i, 0, 0, 0))
        ]
        + [pl.BlockSpec((BV, CHUNKS * W), lambda i, *s: (i, 0))] * NX
        + [whole] * (NX * CHUNKS),
        out_specs=[out] * NX,
        scratch_shapes=[
            pltpu.VMEM((BV, K * BN), jnp.float32),
            pltpu.VMEM((K, BV, BN), jnp.bfloat16),
        ],
    )
    flat = [a for c in sources for a in c]
    return pl.pallas_call(
        foot_kernel,
        grid_spec=spec,
        out_shape=[jax.ShapeDtypeStruct((VLOC, K, rows, BN), jnp.bfloat16)] * NX,
        compiler_params=params(32),
        cost_estimate=cost(4 * VLOC * BV * K * BN * 1024, 6 << 20),
    )(inc, counts, where, footprints, *movies, *flat)


def join_kernel(where, *refs):
    out = refs[NX]
    for t in range(NX):
        out[pl.ds(jnp.bitwise_xor(where[2], t) * VLOC, VLOC)] = refs[t][...]


def join(where, parts):
    shape = jax.ShapeDtypeStruct((VB, K, BV // NX, BN), jnp.bfloat16)
    return whole_call(join_kernel, [shape], 1, NX, [], 16, 2 << 20)(where, *parts)[0]


UP = [(i, (i + 1) % NZ) for i in range(NZ)]
DOWN = [(i, (i - 1) % NZ) for i in range(NZ)]


def ring_gather(own):
    half = OWNED // 2
    ups, downs = [own], [own]
    for _ in range(NZ // 2 - 1):
        ups.append(lax.ppermute(ups[-1], "z", UP))
        downs.append(lax.ppermute(downs[-1], "z", DOWN))
    p4 = lax.ppermute(ups[-1][:half], "z", UP)
    m4 = lax.ppermute(downs[-1][half:], "z", DOWN)
    return (own, *ups[1:], p4, *downs[1:], m4)


def ring_sum(parts):
    half = OWNED // 2
    f32 = jnp.float32
    up = lax.ppermute(parts[4][:half], "z", UP)
    down = lax.ppermute(parts[4][half:], "z", DOWN)
    up = jnp.concatenate([parts[3][:half].astype(f32) + up.astype(f32), parts[3][half:].astype(f32)])
    down = jnp.concatenate(
        [parts[5][:half].astype(f32), parts[5][half:].astype(f32) + down.astype(f32)]
    )
    for above, below in ((2, 6), (1, 7)):
        up = lax.ppermute(up.astype(jnp.bfloat16), "z", UP)
        down = lax.ppermute(down.astype(jnp.bfloat16), "z", DOWN)
        up = up.astype(f32) + parts[above].astype(f32)
        down = down.astype(f32) + parts[below].astype(f32)
    up = lax.ppermute(up.astype(jnp.bfloat16), "z", UP)
    down = lax.ppermute(down.astype(jnp.bfloat16), "z", DOWN)
    return parts[0] + up.astype(f32) + down.astype(f32)


def plane_swap(parts):
    out = [parts[0]]
    for s in range(1, PLANE):
        out.append(lax.ppermute(parts[s], ("y", "c"), [(i, i ^ s) for i in range(PLANE)]))
    return out


def frame_swap(parts):
    out = [parts[0]]
    for t in range(1, NX):
        out.append(lax.ppermute(parts[t], "x", [(i, i ^ t) for i in range(NX)]))
    return out


def body(data, footprints, traces, incidence, counts):
    z = lax.axis_index("z")
    p = lax.axis_index("y") * NC + lax.axis_index("c")
    x = lax.axis_index("x")
    where = jnp.stack([p, z, x]).astype(jnp.int32)
    here = z * PLANE + p
    per_device = incidence.reshape(NZ * PLANE, ENTRIES)
    plane_inc = lax.dynamic_slice_in_dim(per_device, z * PLANE, PLANE)
    inc = lax.dynamic_slice_in_dim(per_device, here, 1).reshape(ENTRIES)
    depth = jnp.arange(NZ, dtype=jnp.int32)
    wanted = ((z + depth) % NZ) * PLANE
    hit = (plane_inc // OWNED)[:, None, :] == (wanted + p)[None, :, None]
    sel = (jnp.sum(jnp.where(hit, plane_inc[:, None, :] % OWNED + 1, 0), axis=2) - 1).reshape(-1)
    column = jnp.arange(PLANE, dtype=jnp.int32)
    mine = (inc // OWNED)[None, None, :] == (wanted[None, :] + column[:, None])[:, :, None]
    entry = jnp.arange(ENTRIES, dtype=jnp.int32)
    ent = jnp.sum(jnp.where(mine, entry, 0), axis=2).reshape(-1)

    flipped, dterm = prep(footprints)
    owner = jnp.arange(NZ * PLANE, dtype=jnp.int32)
    dhit = (owner[:, None] == (inc // OWNED)[None, :]).astype(jnp.float32)
    dslots = jnp.dot(dhit, dterm.reshape(ENTRIES, BN), precision=highest)
    darrived = lax.all_to_all(dslots, ("z", "y", "c"), 0, 0, tiled=True)
    own_blocks = here * OWNED + jnp.arange(OWNED, dtype=jnp.int32)
    named = jnp.sum(
        (per_device[None, :, :] == own_blocks[:, None, None]).astype(jnp.float32), axis=2
    )
    denom = jnp.dot(named, darrived, precision=highest)
    own_counts = lax.dynamic_slice_in_dim(counts, here * OWNED, OWNED)
    live = jnp.arange(BN, dtype=jnp.int32)[None, :] < own_counts[:, None]

    rows = VLOC * BV
    movies = frame_swap(
        [lax.dynamic_slice_in_dim(data, (x ^ t) * rows, rows) for t in range(NX)]
    )

    own = [traces[:, :, c * W : (c + 1) * W] for c in range(CHUNKS)]
    fresh, sources = [], []
    for c in range(CHUNKS):
        arrived = plane_swap(select(sel, where, ring_gather(own[c])))
        sent = plane_swap(terms(c, inc, counts, ent, where, data, footprints, flipped, arrived))
        grad = ring_sum(sum_terms(sel, where, sent))
        updated = jnp.maximum(own[c].astype(jnp.float32) + grad / denom[:, :, None], 0.0)
        new = jnp.where(live[:, :, None], updated, 0.0).astype(jnp.bfloat16)
        fresh.append(new)
        arrived = plane_swap(select(sel, where, ring_gather(new)))
        sources.append(frame_swap(pack(inc, where, arrived)))
    new_traces = jnp.concatenate(fresh, axis=2)
    tiles = foot(inc, counts, where, footprints, movies, sources)
    return new_traces, join(where, frame_swap(tiles))


def solution(mesh):
    fine = Mesh(mesh.devices.reshape(NZ, NY, NC, NX), ("z", "y", "c", "x"))
    vox = ("z", "y", "c")
    placed = (P(vox, "x"), P(vox, None, None, None), P(vox, None, "x"), P(), P())
    return jax.shard_map(
        body,
        mesh=fine,
        in_specs=placed,
        out_specs=(P(vox, None, "x"), P(vox, None, "x", None)),
        check_vma=False,
    )
```

```python
import jax
import jax.numpy as jnp
from jax import lax
from jax.experimental import pallas as pl
from jax.experimental.pallas import tpu as pltpu
from jax.sharding import Mesh
from jax.sharding import PartitionSpec as P

NZ, NY, NC, NX = 8, 4, 2, 4
PLANE = NY * NC
OWNED = 8
BN = 128
BV = 512
K = 4
VB = 8
ENTRIES = VB * K
W = 128
CHUNKS = 2
VLOC = VB // NX
ELOC = VLOC * K

VM = pl.BlockSpec(memory_space=pltpu.VMEM)
SM = pl.BlockSpec(memory_space=pltpu.SMEM)
highest = lax.Precision.HIGHEST


def params(mib):
    return pltpu.CompilerParams(vmem_limit_bytes=mib * 2**20)


def cost(flops, nbytes):
    return pl.CostEstimate(flops=flops, bytes_accessed=nbytes, transcendentals=0)


def whole_call(kernel, out_shape, n_smem, n_vmem, scratch, mib, nbytes):
    out_specs = [VM] * len(out_shape)
    return pl.pallas_call(
        kernel,
        out_shape=out_shape,
        in_specs=[SM] * n_smem + [VM] * n_vmem,
        out_specs=out_specs,
        scratch_shapes=scratch,
        compiler_params=params(mib),
        cost_estimate=cost(0, nbytes),
    )


def blocks(n):
    return jax.ShapeDtypeStruct((n, BN, W), jnp.bfloat16)


def after(array, others):
    def kernel(*refs):
        pass

    anywhere = pl.BlockSpec(memory_space=pl.ANY)
    return pl.pallas_call(
        kernel,
        out_shape=jax.ShapeDtypeStruct(array.shape, array.dtype),
        in_specs=[anywhere] * (1 + len(others)),
        out_specs=anywhere,
        input_output_aliases={0: 0},
        compiler_params=params(16),
    )(array, *others)


def select_kernel(sel, own, p1, p2, p3, p4, m1, m2, m3, m4, out):
    by_r = (own, m1, m2, m3, None, p3, p2, p1)
    half = OWNED // 2
    for q in range(PLANE):
        for r in range(NZ):
            at = q * NZ + r
            b = jnp.maximum(sel[at], 0)
            if r == NZ // 2:
                low = b < half

                @pl.when(low)
                def _():
                    out[at] = p4[b]

                @pl.when(jnp.logical_not(low))
                def _():
                    out[at] = m4[b - half]
            else:
                out[at] = by_r[r][b]


def select(sel, ring):
    shape = [blocks(PLANE * NZ)]
    return whole_call(select_kernel, shape, 1, len(ring), [], 16, 4 << 20)(sel, *ring)[0]


def slot_of(j, where):
    owner = lax.shift_right_logical(j, 3)
    r = jnp.bitwise_and(lax.shift_right_logical(owner, 3) - where[1], NZ - 1)
    return jnp.bitwise_and(owner, PLANE - 1) * NZ + r


def prep_kernel(f_ref, ft_ref, d_ref):
    rowsum = jnp.zeros((BV, 1), jnp.float32)
    for k in range(K):
        tile = f_ref[0, k]
        ft_ref[0, k] = tile.T
        rowsum = rowsum + jnp.sum(tile.astype(jnp.float32), axis=1, keepdims=True)
    for k in range(K):
        d_ref[0, k : k + 1, :] = jnp.sum(
            f_ref[0, k].astype(jnp.float32) * rowsum, axis=0, keepdims=True
        )


def prep(footprints):
    return pl.pallas_call(
        prep_kernel,
        grid=(VB,),
        in_specs=[pl.BlockSpec((1, K, BV, BN), lambda v: (v, 0, 0, 0))],
        out_specs=[
            pl.BlockSpec((1, K, BN, BV), lambda v: (v, 0, 0, 0)),
            pl.BlockSpec((1, K, BN), lambda v: (v, 0, 0)),
        ],
        out_shape=[
            jax.ShapeDtypeStruct((VB, K, BN, BV), jnp.bfloat16),
            jax.ShapeDtypeStruct((VB, K, BN), jnp.float32),
        ],
        compiler_params=params(16),
        cost_estimate=cost(4 * VB * K * BV * BN, 8 << 20),
    )(footprints)


def terms_kernel(inc, counts, ent, where, d_ref, f_ref, ft_ref, held, out, made):
    v = pl.program_id(0)
    neuron = lax.broadcasted_iota(jnp.int32, (BN, W), 0)
    parts = []
    for k in range(K):
        j = inc[v * K + k]
        got = held[slot_of(j, where)]
        parts.append(jnp.where(neuron < counts[j], got, jnp.zeros((), jnp.bfloat16)))
    t_cat = jnp.concatenate(parts, axis=0)
    f_cat = jnp.concatenate([f_ref[0, k] for k in range(K)], axis=1)
    recon = jnp.dot(f_cat, t_cat, preferred_element_type=jnp.float32)
    resid = (d_ref[...].astype(jnp.float32) - recon).astype(jnp.bfloat16)
    ft_cat = ft_ref[0].reshape(K * BN, BV)
    term = jnp.dot(ft_cat, resid, preferred_element_type=jnp.float32)
    made[pl.ds(v * K, K)] = term.astype(jnp.bfloat16).reshape(K, BN, W)

    @pl.when(v == VB - 1)
    def _():
        for at in range(PLANE * NZ):
            out[at] = made[ent[at]]


def terms(chunk, inc, counts, ent, where, data, footprints, flipped, arrived):
    whole = pl.BlockSpec((PLANE * NZ, BN, W), lambda v: (0, 0, 0))
    return pl.pallas_call(
        terms_kernel,
        grid=(VB,),
        in_specs=[SM] * 4
        + [
            pl.BlockSpec((BV, W), lambda v: (v, chunk)),
            pl.BlockSpec((1, K, BV, BN), lambda v: (v, 0, 0, 0)),
            pl.BlockSpec((1, K, BN, BV), lambda v: (v, 0, 0, 0)),
        ]
        + [whole],
        out_specs=whole,
        out_shape=blocks(PLANE * NZ),
        scratch_shapes=[pltpu.VMEM((ENTRIES, BN, W), jnp.bfloat16)],
        compiler_params=params(24),
        cost_estimate=cost(4 * VB * BV * K * BN * W, 13 << 20),
    )(inc, counts, ent, where, data, footprints, flipped, arrived)


def sum_kernel(sel, arrived, *refs):
    outs, total = refs[:NZ], refs[NZ]
    for r in range(NZ):
        total[...] = jnp.zeros_like(total)
        for s in range(PLANE):
            b = sel[s * NZ + r]

            @pl.when(b >= 0)
            def _():
                total[b] += arrived[s * NZ + r].astype(jnp.float32)

        outs[r][...] = total[...].astype(outs[r].dtype)


def sum_terms(sel, arrived):
    shapes = [jax.ShapeDtypeStruct((OWNED, BN, W), jnp.float32)] + [blocks(OWNED)] * (NZ - 1)
    scratch = [pltpu.VMEM((OWNED, BN, W), jnp.float32)]
    return whole_call(sum_kernel, shapes, 1, 1, scratch, 16, 5 << 20)(sel, arrived)


def pack_kernel(inc, where, held, *outs):
    for t in range(NX):
        first = jnp.bitwise_xor(where[2], t) * ELOC
        for i in range(ELOC):
            outs[t][i] = held[slot_of(inc[first + i], where)]


def pack(inc, where, arrived):
    return whole_call(pack_kernel, [blocks(ELOC)] * NX, 2, 1, [], 16, 3 << 20)(
        inc, where, arrived
    )


def foot_kernel(inc, counts, where, f_ref, *refs):
    movies = refs[:NX]
    sources = [refs[NX + c * NX : NX + (c + 1) * NX] for c in range(CHUNKS)]
    outs = refs[NX + CHUNKS * NX : NX + CHUNKS * NX + NX]
    total, moved = refs[NX + CHUNKS * NX + NX :]
    i = pl.program_id(0)
    f_cat = jnp.concatenate([f_ref[0, k] for k in range(K)], axis=1)
    powers = [jnp.zeros((BN, 1), jnp.float32) for _ in range(K)]
    for t in range(NX):
        wide = []
        for k in range(K):
            row = jnp.concatenate([sources[c][t][i * K + k] for c in range(CHUNKS)], axis=1)
            row32 = row.astype(jnp.float32)
            powers[k] = powers[k] + jnp.sum(row32 * row32, axis=1, keepdims=True)
            wide.append(row)
        t_cat = jnp.concatenate(wide, axis=0)
        recon = jnp.dot(f_cat, t_cat, preferred_element_type=jnp.float32)
        movie = movies[t][...]
        resid = (movie.astype(jnp.float32) - recon).astype(jnp.bfloat16)
        part = lax.dot_general(
            resid, t_cat, (((1,), (1,)), ((), ())), preferred_element_type=jnp.float32
        )
        if t == 0:
            total[...] = part
        else:
            total[...] += part
    neuron = lax.broadcasted_iota(jnp.int32, (1, BN), 1)
    for k in range(K):
        power = jnp.broadcast_to(powers[k], (BN, BN)).T[0:1, :]
        alive = neuron < counts[inc[where[2] * ELOC + i * K + k]]
        tile = f_ref[0, k]
        fgrad = total[:, k * BN : (k + 1) * BN]
        tile32 = tile.astype(jnp.float32)
        new = jnp.maximum(tile32 + fgrad / jnp.maximum(power, 1.0), 0.0)
        keep = jnp.logical_and(tile32 > 0, alive)
        moved[k] = jnp.where(keep, new, 0.0).astype(jnp.bfloat16)
    rows = BV // NX
    for t in range(NX):
        start = pl.multiple_of(jnp.bitwise_xor(where[2], t) * rows, rows)
        outs[t][0] = moved[:, pl.ds(start, rows), :]


def foot(inc, counts, where, footprints, movies, sources):
    rows = BV // NX
    whole = pl.BlockSpec((ELOC, BN, W), lambda i, *s: (0, 0, 0))
    out = pl.BlockSpec((1, K, rows, BN), lambda i, *s: (i, 0, 0, 0))
    spec = pltpu.PrefetchScalarGridSpec(
        num_scalar_prefetch=3,
        grid=(VLOC,),
        in_specs=[
            pl.BlockSpec((1, K, BV, BN), lambda i, inc, counts, where: (where[2] * VLOC + i, 0, 0, 0))
        ]
        + [pl.BlockSpec((BV, CHUNKS * W), lambda i, *s: (i, 0))] * NX
        + [whole] * (NX * CHUNKS),
        out_specs=[out] * NX,
        scratch_shapes=[
            pltpu.VMEM((BV, K * BN), jnp.float32),
            pltpu.VMEM((K, BV, BN), jnp.bfloat16),
        ],
    )
    flat = [a for c in sources for a in c]
    return pl.pallas_call(
        foot_kernel,
        grid_spec=spec,
        out_shape=[jax.ShapeDtypeStruct((VLOC, K, rows, BN), jnp.bfloat16)] * NX,
        compiler_params=params(32),
        cost_estimate=cost(4 * VLOC * BV * K * BN * 1024, 6 << 20),
    )(inc, counts, where, footprints, *movies, *flat)


def join_kernel(where, *refs):
    out = refs[NX]
    for t in range(NX):
        out[pl.ds(jnp.bitwise_xor(where[2], t) * VLOC, VLOC)] = refs[t][...]


def join(where, parts):
    shape = jax.ShapeDtypeStruct((VB, K, BV // NX, BN), jnp.bfloat16)
    return whole_call(join_kernel, [shape], 1, NX, [], 16, 2 << 20)(where, *parts)[0]


UP = [(i, (i + 1) % NZ) for i in range(NZ)]
DOWN = [(i, (i - 1) % NZ) for i in range(NZ)]


def ring_gather(own):
    half = OWNED // 2
    ups, downs = [own], [own]
    for _ in range(NZ // 2 - 1):
        ups.append(lax.ppermute(ups[-1], "z", UP))
        downs.append(lax.ppermute(downs[-1], "z", DOWN))
    p4 = lax.ppermute(ups[-1][:half], "z", UP)
    m4 = lax.ppermute(downs[-1][half:], "z", DOWN)
    return (own, *ups[1:], p4, *downs[1:], m4)


def ring_sum(parts):
    half = OWNED // 2
    f32 = jnp.float32
    up = lax.ppermute(parts[4][:half], "z", UP)
    down = lax.ppermute(parts[4][half:], "z", DOWN)
    up = jnp.concatenate([parts[3][:half].astype(f32) + up.astype(f32), parts[3][half:].astype(f32)])
    down = jnp.concatenate(
        [parts[5][:half].astype(f32), parts[5][half:].astype(f32) + down.astype(f32)]
    )
    for above, below in ((2, 6), (1, 7)):
        up = lax.ppermute(up.astype(jnp.bfloat16), "z", UP)
        down = lax.ppermute(down.astype(jnp.bfloat16), "z", DOWN)
        up = up.astype(f32) + parts[above].astype(f32)
        down = down.astype(f32) + parts[below].astype(f32)
    up = lax.ppermute(up.astype(jnp.bfloat16), "z", UP)
    down = lax.ppermute(down.astype(jnp.bfloat16), "z", DOWN)
    return parts[0] + up.astype(f32) + down.astype(f32)


def plane_swap(a):
    return lax.all_to_all(a, ("y", "c"), split_axis=0, concat_axis=0, tiled=True)


def frame_swap(parts):
    out = [parts[0]]
    for t in range(1, NX):
        out.append(lax.ppermute(parts[t], "x", [(i, i ^ t) for i in range(NX)]))
    return out


def body(data, footprints, traces, incidence, counts):
    z = lax.axis_index("z")
    p = lax.axis_index("y") * NC + lax.axis_index("c")
    x = lax.axis_index("x")
    where = jnp.stack([p, z, x]).astype(jnp.int32)
    here = z * PLANE + p
    per_device = incidence.reshape(NZ * PLANE, ENTRIES)
    plane_inc = lax.dynamic_slice_in_dim(per_device, z * PLANE, PLANE)
    inc = lax.dynamic_slice_in_dim(per_device, here, 1).reshape(ENTRIES)
    depth = jnp.arange(NZ, dtype=jnp.int32)
    wanted = ((z + depth) % NZ) * PLANE
    hit = (plane_inc // OWNED)[:, None, :] == (wanted + p)[None, :, None]
    sel = (jnp.sum(jnp.where(hit, plane_inc[:, None, :] % OWNED + 1, 0), axis=2) - 1).reshape(-1)
    column = jnp.arange(PLANE, dtype=jnp.int32)
    mine = (inc // OWNED)[None, None, :] == (wanted[None, :] + column[:, None])[:, :, None]
    entry = jnp.arange(ENTRIES, dtype=jnp.int32)
    ent = jnp.sum(jnp.where(mine, entry, 0), axis=2).reshape(-1)

    flipped, dterm = prep(footprints)
    owner = jnp.arange(NZ * PLANE, dtype=jnp.int32)
    dhit = (owner[:, None] == (inc // OWNED)[None, :]).astype(jnp.float32)
    dslots = jnp.dot(dhit, dterm.reshape(ENTRIES, BN), precision=highest)
    darrived = lax.all_to_all(dslots, ("z", "y", "c"), 0, 0, tiled=True)
    own_blocks = here * OWNED + jnp.arange(OWNED, dtype=jnp.int32)
    named = jnp.sum(
        (per_device[None, :, :] == own_blocks[:, None, None]).astype(jnp.float32), axis=2
    )
    denom = jnp.dot(named, darrived, precision=highest)
    own_counts = lax.dynamic_slice_in_dim(counts, here * OWNED, OWNED)
    live = jnp.arange(BN, dtype=jnp.int32)[None, :] < own_counts[:, None]

    rows = VLOC * BV
    movies = frame_swap(
        [lax.dynamic_slice_in_dim(data, (x ^ t) * rows, rows) for t in range(NX)]
    )

    own = [traces[:, :, c * W : (c + 1) * W] for c in range(CHUNKS)]
    fresh, sources = [], []
    for c in range(CHUNKS):
        arrived = plane_swap(select(sel, ring_gather(own[c])))
        sent = plane_swap(terms(c, inc, counts, ent, where, data, footprints, flipped, arrived))
        if c == 0:
            sent = after(sent, movies[1:])
        grad = ring_sum(sum_terms(sel, sent))
        updated = jnp.maximum(own[c].astype(jnp.float32) + grad / denom[:, :, None], 0.0)
        new = jnp.where(live[:, :, None], updated, 0.0).astype(jnp.bfloat16)
        fresh.append(new)
        arrived = plane_swap(select(sel, ring_gather(new)))
        sources.append(frame_swap(pack(inc, where, arrived)))
    new_traces = jnp.concatenate(fresh, axis=2)
    tiles = foot(inc, counts, where, footprints, movies, sources)
    return new_traces, join(where, frame_swap(tiles))


def solution(mesh):
    fine = Mesh(mesh.devices.reshape(NZ, NY, NC, NX), ("z", "y", "c", "x"))
    vox = ("z", "y", "c")
    placed = (P(vox, "x"), P(vox, None, None, None), P(vox, None, "x"), P(), P())
    return jax.shard_map(
        body,
        mesh=fine,
        in_specs=placed,
        out_specs=(P(vox, None, "x"), P(vox, None, "x", None)),
        check_vma=False,
    )
```
